256 devices in a mesh: section: 16 (over y, z_hi), tp: 16 (over z_lo, x, core).
Axes of the slice: x: 4, y: 4, z: 8 (z_hi: 4, z_lo: 2; z = z_hi * 2 + z_lo), core: 2. Of those that a mesh axis runs over, the one named last changes fastest.
Arguments:
- saved_caches: bfloat16 [16, 2, 2048, 3, 32, 128], P('section', None, 'tp'), may hold values from -100 to 100
- keeper_code: int32 [16], replicated, may hold values from 0 to 3, as said below
- result_slope: bfloat16 [16, 2048, 32, 128], P('section', 'tp'), may hold values from -6 to 6
Outputs:
- stash_grad: bfloat16 [16, 2048, 3, 32, 128], P('section', 'tp')
The draws below stay inside these ranges and needn't reach their ends.
Inputs may be any that keep to these rules, and one draw needn't show every extreme that they name: `keeper_code`: A code below 2 names a slot of the section's own store; a code c of 2 or more names slot c - 2 of the store of section 15 - s. Every code occurs.
All inputs are finite; a program needn't handle non-finite values.
Results may differ from the reference program's by a relative error of at most 0.0073.
Values may be sent and summed in bfloat16 or wider, within the bound.
A program may use at most 128 MiB of HBM per device.

```python
import jax
import jax.numpy as jnp
from jax import lax

HEADS = 32
HD = 128
SLOTS = 2
SEQ = 2048
SECTIONS = 16


def draw_saved_caches(key, part):
    key = jax.random.fold_in(key, 11)
    array_dimensions = (SECTIONS, SLOTS, SEQ, 3, HEADS, HD)
    first = jax.random.fold_in(key, 0)
    base = jnp.clip(jax.random.normal(first, array_dimensions, jnp.float32), -6.0, 6.0)
    return base.astype(jnp.bfloat16)


def draw_keeper_code(key, part):
    key = jax.random.fold_in(key, 23)
    order = jax.random.permutation(key, SECTIONS)
    return (order % (2 * SLOTS)).astype(jnp.int32)


def block_levels(key, extent, cuts, low, high):
    gain, own = 1.0, jax.random.fold_in(key, 6)
    for axis_at, shards_of in cuts:
        steps = jnp.exp(jax.random.uniform(jax.random.fold_in(own, axis_at), (shards_of,), jnp.float32, low / len(cuts), high / len(cuts)))
        gain = gain * jnp.repeat(steps, extent[axis_at] // shards_of).reshape([-1 if axis == axis_at else 1 for axis in range(len(extent))])
    return gain


def bell_draw(rng, shape, width, most, cuts=(), kind=jnp.bfloat16):
    entries = jax.random.normal(rng, shape, jnp.float32) * width
    if len(cuts) > 0:
        entries = block_levels(rng, shape, cuts, -0.22, 0.18) * entries
    return jnp.clip(entries, min=-most, max=most).astype(kind)


def setup_inputs(seed: int = 0) -> dict:
    splits = jax.random.split(jax.random.key(seed), 4)
    saved_caches = draw_saved_caches(jax.random.fold_in(splits[3], 71), 0)
    keeper_code = draw_keeper_code(jax.random.fold_in(splits[3], 71), 0)
    result_slope = bell_draw(splits[2], (SECTIONS, SEQ, HEADS, HD), 1.0, 6.0, ((0, 16), (1, 16)))
    return {"saved_caches": saved_caches, "keeper_code": keeper_code, "result_slope": result_slope}


def head_grads(queries, keys_in, values_in, grads_in):
    scaling = HD ** -0.5
    scores = jnp.dot(queries, keys_in.T, preferred_element_type=jnp.float32) * scaling
    row_ids = lax.broadcasted_iota(jnp.int32, scores.shape, 0)
    col_ids = lax.broadcasted_iota(jnp.int32, scores.shape, 1)
    causal = row_ids >= col_ids
    scores = jnp.where(causal, scores, jnp.float32(-1e30))
    peak = jnp.max(scores, axis=1, keepdims=True)
    expo = jnp.where(causal, jnp.exp(scores - peak), jnp.float32(0.0))
    probability = expo / jnp.sum(expo, axis=1, keepdims=True)
    weights = probability.astype(jnp.bfloat16)
    attended = jnp.dot(weights, values_in, preferred_element_type=jnp.float32)
    value_grad = jnp.dot(weights.T, grads_in, preferred_element_type=jnp.float32)
    prob_grad = jnp.dot(grads_in, values_in.T, preferred_element_type=jnp.float32)
    row_dots = jnp.sum(grads_in.astype(jnp.float32) * attended, axis=1, keepdims=True)
    score_grad = (probability * (prob_grad - row_dots) * scaling).astype(jnp.bfloat16)
    query_grad = jnp.dot(score_grad, keys_in, preferred_element_type=jnp.float32)
    key_grad = jnp.dot(score_grad.T, queries, preferred_element_type=jnp.float32)
    return jnp.stack([query_grad, key_grad, value_grad]).astype(jnp.bfloat16)


def reference(saved_caches, keeper_code, result_slope):
    def one_section(segment_index):
        code = keeper_code[segment_index]
        twin_segment = (SECTIONS - 1 - segment_index).astype(jnp.int32)
        home_keeper = lax.dynamic_index_in_dim(saved_caches, segment_index.astype(jnp.int32), 0, keepdims=False)
        distant_keeper = lax.dynamic_index_in_dim(saved_caches, twin_segment, 0, keepdims=False)
        own_slot = lax.dynamic_index_in_dim(home_keeper, jnp.clip(code, 0, SLOTS - 1).astype(jnp.int32), 0, keepdims=False)
        far_slot = lax.dynamic_index_in_dim(distant_keeper, jnp.clip(code - SLOTS, 0, SLOTS - 1).astype(jnp.int32), 0, keepdims=False)
        chosen = jnp.where(code >= SLOTS, far_slot, own_slot)
        grads_here = lax.dynamic_index_in_dim(result_slope, segment_index.astype(jnp.int32), 0, keepdims=False)
        by_head = jnp.moveaxis(chosen, 2, 0)
        grad_head = jnp.moveaxis(grads_here, 1, 0)

        def per_head(pair):
            triple, grads_in = pair
            return head_grads(triple[:, 0], triple[:, 1], triple[:, 2], grads_in)

        result = lax.map(per_head, (by_head, grad_head))
        return jnp.transpose(result, (2, 1, 0, 3))

    return lax.map(one_section, jnp.arange(SECTIONS, dtype=jnp.int32))
```

```python
import functools

import jax
import jax.numpy as jnp
from jax import lax
from jax.experimental import pallas as pl
from jax.experimental.pallas import tpu as pltpu
from jax.sharding import PartitionSpec as P

MESH = pl.DeviceIdType.MESH
F32 = jnp.float32
BF16 = jnp.bfloat16
LOG2E = 1.4426950408889634
ROWS_BY_ROWS = (((1,), (1,)), ((), ()))
PLAIN = (((1,), (0,)), ((), ()))


def dot(a, b, dims):
    return lax.dot_general(a, b, dims, preferred_element_type=F32)


def head_backward(q, k, v, g, put, scores, slopes, key_total, value_total, k_turned, length, block):
    width = q.shape[-1]
    scaling = width ** (-0.5)
    exponent = scaling * LOG2E
    blocks = length // block
    k_turned[...] = k[...].T
    key_ids = lax.broadcasted_iota(jnp.int32, (block, block), 0)
    query_ids = lax.broadcasted_iota(jnp.int32, (block, block), 1)
    causal = key_ids <= query_ids

    def fold(x, op):
        return op(x.reshape(block // 8, 8, block), axis=0)

    for i in reversed(range(blocks)):
        rows = pl.ds(i * block, block)
        q_rows, g_rows = q[rows, :], g[rows, :]
        peak = jnp.full((8, block), -3.0e38, F32)
        for j in range(i + 1):
            cols = pl.ds(j * block, block)
            s = dot(k[cols, :], q_rows, ROWS_BY_ROWS)
            if j == i:
                s = jnp.where(causal, s, F32(-1e30))
            scores[cols, :] = s
            peak = jnp.maximum(peak, fold(s, jnp.max))
        peak = jnp.max(peak, axis=0, keepdims=True)
        total = jnp.zeros((8, block), F32)
        dots = jnp.zeros((8, block), F32)
        for j in range(i + 1):
            cols = pl.ds(j * block, block)
            e = jnp.exp2((scores[cols, :] - peak) * exponent)
            dp = dot(v[cols, :], g_rows, ROWS_BY_ROWS)
            scores[cols, :] = e
            slopes[cols, :] = dp
            total = total + fold(e, jnp.sum)
            dots = dots + fold(e * dp, jnp.sum)
        inverse = 1.0 / jnp.sum(total, axis=0, keepdims=True)
        row_dots = jnp.sum(dots, axis=0, keepdims=True) * inverse
        query_total = jnp.zeros((width, block), F32)
        for j in range(i + 1):
            cols = pl.ds(j * block, block)
            p = scores[cols, :] * inverse
            ds = (p * (slopes[cols, :] - row_dots)).astype(BF16)
            dv = dot(p.astype(BF16), g_rows, PLAIN)
            dk = dot(ds, q_rows, PLAIN)
            if i == blocks - 1:
                value_total[cols, :] = dv
                key_total[cols, :] = dk
            else:
                value_total[cols, :] += dv
                key_total[cols, :] += dk
            query_total = query_total + dot(k_turned[:, cols], ds, PLAIN)
        put(
            i,
            (query_total.T * scaling).astype(BF16),
            (key_total[rows, :] * scaling).astype(BF16),
            value_total[rows, :].astype(BF16),
        )


def kernel(
    sections, groups, heads, tokens, block,
    flag, far_src, own_src, grad_src, out,
    far, own, grad, sel, done, scores, slopes, key_total, value_total, k_turned,
    far_send, far_recv, own_send, own_recv, grad_send, grad_recv, out_send, out_recv,
):
    s = lax.axis_index("section")
    t = lax.axis_index("tp")
    mirror = sections - 1 - s
    length = groups * tokens
    mine = pl.ds(pl.multiple_of(t * tokens, tokens), tokens)

    barrier = pltpu.get_barrier_semaphore()

    def greet(i, _):
        peer = lax.bitwise_xor(t, i)
        pl.semaphore_signal(barrier, inc=1, device_id=(mirror, peer), device_id_type=MESH)

        @pl.when(i > 0)
        def _():
            pl.semaphore_signal(barrier, inc=1, device_id=(s, peer), device_id_type=MESH)

        return 0

    lax.fori_loop(0, groups, greet, 0)
    pl.semaphore_wait(barrier, 2 * groups - 1)

    def send_far(hd):
        def f(i, _):
            peer = lax.bitwise_xor(t, i)
            pltpu.make_async_remote_copy(
                src_ref=far_src.at[peer, hd], dst_ref=far.at[hd, :, mine, :],
                send_sem=far_send, recv_sem=far_recv.at[hd],
                device_id=(mirror, peer), device_id_type=MESH,
            ).start()
            return 0

        lax.fori_loop(0, groups, f, 0)

    def send_own(hd):
        pltpu.make_async_copy(own_src.at[t, hd], own.at[hd, :, mine, :], own_recv.at[hd]).start()
        pltpu.make_async_copy(grad_src.at[t, hd], grad.at[hd, mine, :], grad_recv.at[hd]).start()

        def f(i, _):
            peer = lax.bitwise_xor(t, i)
            pltpu.make_async_remote_copy(
                src_ref=own_src.at[peer, hd], dst_ref=own.at[hd, :, mine, :],
                send_sem=own_send, recv_sem=own_recv.at[hd],
                device_id=(s, peer), device_id_type=MESH,
            ).start()
            pltpu.make_async_remote_copy(
                src_ref=grad_src.at[peer, hd], dst_ref=grad.at[hd, mine, :],
                send_sem=grad_send, recv_sem=grad_recv.at[hd],
                device_id=(s, peer), device_id_type=MESH,
            ).start()
            return 0

        lax.fori_loop(1, groups, f, 0)

    for hd in range(heads):
        send_far(hd)
        send_own(hd)

    take_far = flag[0] != 0

    def one_head(hd, _):
        pltpu.make_async_copy(own.at[hd], own.at[hd], own_recv.at[hd]).wait()
        pltpu.make_async_copy(grad.at[hd], grad.at[hd], grad_recv.at[hd]).wait()
        pltpu.make_async_copy(far.at[hd], far.at[hd], far_recv.at[hd]).wait()

        def choose(n, _):
            rows = pl.ds(pl.multiple_of(n * block, block), block)
            sel[:, rows, :] = jnp.where(take_far, far[hd, :, rows, :], own[hd, :, rows, :])
            return 0

        lax.fori_loop(0, length // block, choose, 0)

        def put(i, dq, dk, dv):
            per = block // tokens
            for n in range(per):
                part = slice(n * tokens, (n + 1) * tokens)
                done[hd, i * per + n, 0] = dq[part]
                done[hd, i * per + n, 1] = dk[part]
                done[hd, i * per + n, 2] = dv[part]

        head_backward(
            sel.at[0], sel.at[1], sel.at[2], grad.at[hd], put,
            scores, slopes, key_total, value_total, k_turned, length, block,
        )
        pltpu.make_async_copy(done.at[hd, t], out.at[t, hd], out_recv).start()

        def f(i, _):
            peer = lax.bitwise_xor(t, i)
            pltpu.make_async_remote_copy(
                src_ref=done.at[hd, peer], dst_ref=out.at[t, hd],
                send_sem=out_send, recv_sem=out_recv,
                device_id=(s, peer), device_id_type=MESH,
            ).start()
            return 0

        lax.fori_loop(1, groups, f, 0)
        return 0

    lax.fori_loop(0, heads, one_head, 0)

    pltpu.make_async_copy(far_src, far_src, far_send).wait()
    rest = pl.ds(1, groups - 1)
    pltpu.make_async_copy(own_src.at[rest], own_src.at[rest], own_send).wait()
    pltpu.make_async_copy(grad_src.at[rest], grad_src.at[rest], grad_send).wait()
    pltpu.make_async_copy(out.at[rest], out.at[rest], out_send).wait()
    pltpu.make_async_copy(out, out, out_recv).wait()


def solution(mesh):
    sections, groups = mesh.shape["section"], mesh.shape["tp"]

    def local(saved_caches, keeper_code, result_slope):
        slots, tokens, triple, head_count, width = saved_caches.shape[1:]
        heads = head_count // groups
        length = groups * tokens
        block = 256
        s = lax.axis_index("section")
        home = keeper_code[s]
        away = keeper_code[sections - 1 - s]

        def slot(index):
            index = jnp.clip(index, 0, slots - 1)
            x = lax.dynamic_index_in_dim(saved_caches[0], index, 0, keepdims=False)
            x = x.reshape(tokens, triple, groups, heads, width)
            return jnp.transpose(x, (2, 3, 1, 0, 4))

        far_src = slot(away - slots)
        own_src = slot(home)
        grad_src = jnp.transpose(result_slope[0].reshape(tokens, groups, heads, width), (1, 2, 0, 3))
        flag = (home >= slots).astype(jnp.int32).reshape(1)
        anywhere = pl.BlockSpec(memory_space=pl.ANY)
        vmem = pltpu.VMEM
        sem = pltpu.SemaphoreType.DMA
        out = pl.pallas_call(
            functools.partial(kernel, sections, groups, heads, tokens, block),
            out_shape=jax.ShapeDtypeStruct((groups, heads, triple, tokens, width), BF16),
            in_specs=[pl.BlockSpec(memory_space=pltpu.SMEM), anywhere, anywhere, anywhere],
            out_specs=anywhere,
            scratch_shapes=[
                vmem((heads, triple, length, width), BF16),
                vmem((heads, triple, length, width), BF16),
                vmem((heads, length, width), BF16),
                vmem((triple, length, width), BF16),
                vmem((heads, groups, triple, tokens, width), BF16),
                vmem((length, block), F32),
                vmem((length, block), F32),
                vmem((length, width), F32),
                vmem((length, width), F32),
                vmem((width, length), BF16),
                sem, sem((heads,)), sem, sem((heads,)), sem, sem((heads,)), sem, sem,
            ],
            compiler_params=pltpu.CompilerParams(
                collective_id=0, has_side_effects=True, vmem_limit_bytes=48 * 2**20
            ),
        )(flag, far_src, own_src, grad_src)
        return jnp.transpose(out, (3, 2, 0, 1, 4)).reshape(1, tokens, triple, head_count, width)

    return jax.shard_map(
        local,
        mesh=mesh,
        in_specs=(P("section", None, "tp", None, None, None), P(), P("section", "tp", None, None)),
        out_specs=P("section", "tp", None, None, None),
        check_vma=False,
    )
```

```python
import functools

import jax
import jax.numpy as jnp
from jax import lax
from jax.experimental import pallas as pl
from jax.experimental.pallas import tpu as pltpu
from jax.sharding import PartitionSpec as P

MESH = pl.DeviceIdType.MESH
F32 = jnp.float32
BF16 = jnp.bfloat16
LOG2E = 1.4426950408889634
ROWS_BY_ROWS = (((1,), (1,)), ((), ()))
PLAIN = (((1,), (0,)), ((), ()))


def dot(a, b, dims):
    return lax.dot_general(a, b, dims, preferred_element_type=F32)


def fold(x, op):
    return op(x.reshape(x.shape[0] // 8, 8, x.shape[1]), axis=0)


def place(i, j):
    return i * (i + 1) // 2 + j


def softmax_and_value_grad(q, k, g, probs, value_total, put, length, block):
    exponent = q.shape[-1] ** (-0.5) * LOG2E
    blocks = length // block
    key_ids = lax.broadcasted_iota(jnp.int32, (block, block), 0)
    query_ids = lax.broadcasted_iota(jnp.int32, (block, block), 1)
    causal = key_ids <= query_ids
    for i in reversed(range(blocks)):
        rows = pl.ds(i * block, block)
        q_rows, g_rows = q[rows, :], g[rows, :]
        peak = jnp.full((8, block), -3.0e38, F32)
        for j in range(i + 1):
            s = dot(k[pl.ds(j * block, block), :], q_rows, ROWS_BY_ROWS)
            if j == i:
                s = jnp.where(causal, s, F32(-1e30))
            probs[place(i, j)] = s
            peak = jnp.maximum(peak, fold(s, jnp.max))
        peak = jnp.max(peak, axis=0, keepdims=True)
        total = jnp.zeros((8, block), F32)
        for j in range(i + 1):
            e = jnp.exp2((probs[place(i, j)] - peak) * exponent)
            probs[place(i, j)] = e
            total = total + fold(e, jnp.sum)
        inverse = 1.0 / jnp.sum(total, axis=0, keepdims=True)
        for j in range(i + 1):
            cols = pl.ds(j * block, block)
            p = probs[place(i, j)] * inverse
            probs[place(i, j)] = p
            dv = dot(p.astype(BF16), g_rows, PLAIN)
            if i == blocks - 1:
                value_total[cols, :] = dv
            else:
                value_total[cols, :] += dv
        put(i, value_total[rows, :].astype(BF16))


def query_and_key_grad(q, k, v, g, probs, slopes, key_total, k_turned, put, length, block, which):
    width = q.shape[-1]
    scaling = width ** (-0.5)
    blocks = length // block
    for i in which:
        rows = pl.ds(i * block, block)
        q_rows, g_rows = q[rows, :], g[rows, :]
        dots = jnp.zeros((8, block), F32)
        for j in range(i + 1):
            cols = pl.ds(j * block, block)
            dp = dot(v[cols, :], g_rows, ROWS_BY_ROWS)
            slopes[cols, :] = dp
            dots = dots + fold(probs[place(i, j)] * dp, jnp.sum)
        row_dots = jnp.sum(dots, axis=0, keepdims=True)
        query_total = jnp.zeros((width, block), F32)
        for j in range(i + 1):
            cols = pl.ds(j * block, block)
            ds = (probs[place(i, j)] * (slopes[cols, :] - row_dots)).astype(BF16)
            dk = dot(ds, q_rows, PLAIN)
            if i == blocks - 1:
                key_total[cols, :] = dk
            else:
                key_total[cols, :] += dk
            query_total = query_total + dot(k_turned[:, cols], ds, PLAIN)
        put(i, (query_total.T * scaling).astype(BF16), (key_total[rows, :] * scaling).astype(BF16))


def kernel(
    sections, groups, heads, tokens, block, slots,
    codes, store, slope, out,
    store_in0, store_in1, store_in2, slope_in, far_out, own_out, grad_out,
    far, own, grad, sel, done, probs, slopes, key_total, value_total, k_turned,
    load_sem, far_send, far_recv, own_send, own_recv, grad_send, grad_recv, out_send, out_recv,
):
    s = lax.axis_index("section")
    t = lax.axis_index("tp")
    mirror = sections - 1 - s
    length = groups * tokens
    triple = store.shape[2]
    mine = pl.ds(pl.multiple_of(t * tokens, tokens), tokens)
    step = 16
    store_in = (store_in0, store_in1, store_in2)

    def load(w):
        return pltpu.make_async_copy(store.at[:, :, w], store_in[w], load_sem.at[w])

    def load_slope():
        return pltpu.make_async_copy(slope, slope_in, load_sem.at[triple])

    for w in range(triple):
        load(w).start()
    load_slope().start()

    barrier = pltpu.get_barrier_semaphore()

    def greet(i, _):
        peer = lax.bitwise_xor(t, i)
        pl.semaphore_signal(barrier, inc=1, device_id=(mirror, peer), device_id_type=MESH)

        @pl.when(i > 0)
        def _():
            pl.semaphore_signal(barrier, inc=1, device_id=(s, peer), device_id_type=MESH)

        return 0

    lax.fori_loop(0, groups, greet, 0)
    home = codes[s]
    away = codes[mirror]
    own_slot = jnp.clip(home, 0, slots - 1)
    far_slot = jnp.clip(away - slots, 0, slots - 1)
    take_far = home >= slots

    def by_head(slot, w, to):
        def f(n, _):
            rows = pl.ds(pl.multiple_of(n * step, step), step)
            to[w, :, rows, :] = jnp.swapaxes(store_in[w][slot, rows], 0, 1)
            return 0

        lax.fori_loop(0, tokens // step, f, 0)

    def each_peer(first, f):
        def g(i, _):
            f(lax.bitwise_xor(t, i))
            return 0

        lax.fori_loop(first, groups, g, 0)

    def send_far(hd, w):
        def f(peer):
            pltpu.make_async_remote_copy(
                src_ref=far_out.at[w, peer * heads + hd], dst_ref=far.at[hd, w, mine, :],
                send_sem=far_send.at[hd, w], recv_sem=far_recv.at[hd, w],
                device_id=(mirror, peer), device_id_type=MESH,
            ).start()

        each_peer(0, f)

    def far_sent(hd, w):
        some = pl.ds(0, groups)
        pltpu.make_async_copy(far_out.at[w, some], far_out.at[w, some], far_send.at[hd, w]).wait()

    def far_here(hd, w):
        pltpu.make_async_copy(far.at[hd, w], far.at[hd, w], far_recv.at[hd, w]).wait()

    def send_own(hd):
        pltpu.make_async_copy(own_out.at[:, t * heads + hd], own.at[hd, :, mine, :], own_recv.at[hd]).start()
        pltpu.make_async_copy(grad_out.at[t * heads + hd], grad.at[hd, mine, :], grad_recv.at[hd]).start()

        def f(peer):
            pltpu.make_async_remote_copy(
                src_ref=own_out.at[:, peer * heads + hd], dst_ref=own.at[hd, :, mine, :],
                send_sem=own_send, recv_sem=own_recv.at[hd],
                device_id=(s, peer), device_id_type=MESH,
            ).start()
            pltpu.make_async_remote_copy(
                src_ref=grad_out.at[peer * heads + hd], dst_ref=grad.at[hd, mine, :],
                send_sem=grad_send, recv_sem=grad_recv.at[hd],
                device_id=(s, peer), device_id_type=MESH,
            ).start()

        each_peer(1, f)

    late = pl.ds(triple - 1, 1)
    early = pl.ds(0, triple - 1)
    last = triple - 1

    def slope_by_head(n, _):
        rows = pl.ds(pl.multiple_of(n * step, step), step)
        grad_out[:, rows, :] = jnp.swapaxes(slope_in[rows], 0, 1)
        return 0

    load(1).wait()
    by_head(far_slot, 1, far_out)
    pl.semaphore_wait(barrier, 2 * groups - 1)
    send_far(0, 1)
    load(0).wait()
    by_head(far_slot, 0, far_out)
    send_far(0, 0)
    load_slope().wait()
    lax.fori_loop(0, tokens // step, slope_by_head, 0)
    load(last).wait()
    for w in range(triple):
        by_head(own_slot, w, own_out)
    send_own(0)
    by_head(far_slot, last, far_out)
    send_far(0, last)
    for hd in range(1, heads):
        for w in (1, 0, last):
            send_far(hd, w)
        send_own(hd)

    def one_head(hd, _):
        pltpu.make_async_copy(own.at[hd], own.at[hd], own_recv.at[hd]).wait()
        pltpu.make_async_copy(grad.at[hd], grad.at[hd], grad_recv.at[hd]).wait()
        far_here(hd, 1)
        far_here(hd, 0)

        def choose(ws):
            def f(n, _):
                rows = pl.ds(pl.multiple_of(n * block, block), block)
                sel[ws, rows, :] = jnp.where(take_far, far[hd, ws, rows, :], own[hd, ws, rows, :])
                return 0

            lax.fori_loop(0, length // block, f, 0)

        per = block // tokens

        def put_value(i, dv):
            for n in range(per):
                done[hd, i * per + n, 2] = dv[n * tokens:(n + 1) * tokens]

        def put_query_key(i, dq, dk):
            for n in range(per):
                done[hd, i * per + n, 0] = dq[n * tokens:(n + 1) * tokens]
                done[hd, i * per + n, 1] = dk[n * tokens:(n + 1) * tokens]

        def give(peer, ws):
            @pl.when(peer == t)
            def _():
                pltpu.make_async_copy(done.at[hd, peer, ws], out.at[t, hd, ws], out_recv).start()

            @pl.when(peer != t)
            def _():
                pltpu.make_async_remote_copy(
                    src_ref=done.at[hd, peer, ws], dst_ref=out.at[t, hd, ws],
                    send_sem=out_send, recv_sem=out_recv,
                    device_id=(s, peer), device_id_type=MESH,
                ).start()

        choose(early)
        q, k, v, g = sel.at[0], sel.at[1], sel.at[2], grad.at[hd]
        k_turned[...] = k[...].T
        softmax_and_value_grad(q, k, g, probs, value_total, put_value, length, block)
        each_peer(0, lambda peer: give(peer, late))
        far_here(hd, last)
        choose(late)
        blocks = length // block
        half = groups // 2
        for part in (1, 0):
            which = reversed(range(part * blocks // 2, (part + 1) * blocks // 2))
            query_and_key_grad(
                q, k, v, g, probs, slopes, key_total, k_turned, put_query_key, length, block, which
            )

            def f(n, _):
                give(part * half + lax.rem(lax.bitwise_xor(t, n), half), early)
                return 0

            lax.fori_loop(0, half, f, 0)
        return 0

    lax.fori_loop(0, heads, one_head, 0)

    for hd in range(heads):
        for w in range(triple):
            far_sent(hd, w)
    sent = pl.ds(0, (groups - 1) * heads)
    pltpu.make_async_copy(own_out.at[:, sent], own_out.at[:, sent], own_send).wait()
    pltpu.make_async_copy(grad_out.at[sent], grad_out.at[sent], grad_send).wait()
    rest = pl.ds(1, groups - 1)
    pltpu.make_async_copy(out.at[rest], out.at[rest], out_send).wait()
    pltpu.make_async_copy(out, out, out_recv).wait()


def by_token(parts, whole, came, turned, load_sem, store_sem):
    groups, heads, triple, tokens, width = parts.shape
    step = 16
    loads = [pltpu.make_async_copy(parts.at[:, :, w], came.at[w], load_sem.at[w]) for w in range(triple)]
    stores = [pltpu.make_async_copy(turned.at[w], whole.at[:, w], store_sem.at[w]) for w in range(triple)]
    for load in loads:
        load.start()
    for w in range(triple):
        loads[w].wait()
        for n in range(tokens // step):
            rows = pl.ds(n * step, step)
            piece = came[w, :, :, rows, :].reshape(groups * heads, step, width)
            turned[w, rows] = jnp.swapaxes(piece, 0, 1)
        stores[w].start()
    for store in stores:
        store.wait()


def solution(mesh):
    sections, groups = mesh.shape["section"], mesh.shape["tp"]

    def local(saved_caches, keeper_code, result_slope):
        slots, tokens, triple, head_count, width = saved_caches.shape[1:]
        heads = head_count // groups
        length = groups * tokens
        block = 256
        blocks = length // block
        anywhere = pl.BlockSpec(memory_space=pl.ANY)
        vmem = pltpu.VMEM
        sem = pltpu.SemaphoreType.DMA
        out = pl.pallas_call(
            functools.partial(kernel, sections, groups, heads, tokens, block, slots),
            out_shape=jax.ShapeDtypeStruct((groups, heads, triple, tokens, width), BF16),
            in_specs=[pl.BlockSpec(memory_space=pltpu.SMEM), anywhere, anywhere],
            out_specs=anywhere,
            scratch_shapes=[
                *[vmem((slots, tokens, head_count, width), BF16)] * triple,
                vmem((tokens, head_count, width), BF16),
                vmem((triple, head_count, tokens, width), BF16),
                vmem((triple, head_count, tokens, width), BF16),
                vmem((head_count, tokens, width), BF16),
                vmem((heads, triple, length, width), BF16),
                vmem((heads, triple, length, width), BF16),
                vmem((heads, length, width), BF16),
                vmem((triple, length, width), BF16),
                vmem((heads, groups, triple, tokens, width), BF16),
                vmem((place(blocks, 0), block, block), F32),
                vmem((length, block), F32),
                vmem((length, width), F32),
                vmem((length, width), F32),
                vmem((width, length), BF16),
                sem((triple + 1,)),
                sem((heads, triple)), sem((heads, triple)), sem, sem((heads,)), sem, sem((heads,)), sem, sem,
            ],
            compiler_params=pltpu.CompilerParams(
                collective_id=0, has_side_effects=True, vmem_limit_bytes=56 * 2**20
            ),
        )(keeper_code, saved_caches[0], result_slope[0])
        whole = pl.pallas_call(
            by_token,
            out_shape=jax.ShapeDtypeStruct((tokens, triple, head_count, width), BF16),
            in_specs=[anywhere],
            out_specs=anywhere,
            scratch_shapes=[
                vmem((triple, groups, heads, tokens, width), BF16),
                vmem((triple, tokens, head_count, width), BF16),
                sem((triple,)), sem((triple,)),
            ],
            compiler_params=pltpu.CompilerParams(vmem_limit_bytes=56 * 2**20),
        )(out)
        return whole[None]

    return jax.shard_map(
        local,
        mesh=mesh,
        in_specs=(P("section", None, "tp", None, None, None), P(), P("section", "tp", None, None)),
        out_specs=P("section", "tp", None, None, None),
        check_vma=False,
    )
```

```python
import functools

import jax
import jax.numpy as jnp
from jax import lax
from jax.experimental import pallas as pl
from jax.experimental.pallas import tpu as pltpu
from jax.sharding import PartitionSpec as P

MESH = pl.DeviceIdType.MESH
F32 = jnp.float32
BF16 = jnp.bfloat16
LOG2E = 1.4426950408889634
ROWS_BY_ROWS = (((1,), (1,)), ((), ()))
PLAIN = (((1,), (0,)), ((), ()))


def dot(a, b, dims):
    return lax.dot_general(a, b, dims, preferred_element_type=F32)


def fold(x, op):
    return op(x.reshape(x.shape[0] // 8, 8, x.shape[1]), axis=0)


def chips_first(n):
    return n % 4 * 2 + n // 4 % 2 + n // 8 * 8


def place(i, j):
    return i * (i + 1) // 2 + j


def softmax_and_value_grad(q, k, g, probs, value_total, put, length, block):
    exponent = q.shape[-1] ** (-0.5) * LOG2E
    blocks = length // block
    key_ids = lax.broadcasted_iota(jnp.int32, (block, block), 0)
    query_ids = lax.broadcasted_iota(jnp.int32, (block, block), 1)
    causal = key_ids <= query_ids
    for i in reversed(range(blocks)):
        rows = pl.ds(i * block, block)
        q_rows, g_rows = q[rows, :], g[rows, :]
        peak = jnp.full((8, block), -3.0e38, F32)
        for j in range(i + 1):
            s = dot(k[pl.ds(j * block, block), :], q_rows, ROWS_BY_ROWS)
            if j == i:
                s = jnp.where(causal, s, F32(-1e30))
            probs[place(i, j)] = s
            peak = jnp.maximum(peak, fold(s, jnp.max))
        peak = jnp.max(peak, axis=0, keepdims=True)
        total = jnp.zeros((8, block), F32)
        for j in range(i + 1):
            e = jnp.exp2((probs[place(i, j)] - peak) * exponent)
            probs[place(i, j)] = e
            total = total + fold(e, jnp.sum)
        inverse = 1.0 / jnp.sum(total, axis=0, keepdims=True)
        for j in range(i + 1):
            cols = pl.ds(j * block, block)
            p = probs[place(i, j)] * inverse
            probs[place(i, j)] = p
            dv = dot(p.astype(BF16), g_rows, PLAIN)
            if i == blocks - 1:
                value_total[cols, :] = dv
            else:
                value_total[cols, :] += dv
        put(i, value_total[rows, :].astype(BF16))


def query_and_key_grad(q, k, v, g, probs, slopes, key_total, k_turned, put, length, block, which):
    width = q.shape[-1]
    scaling = width ** (-0.5)
    blocks = length // block
    for i in which:
        rows = pl.ds(i * block, block)
        q_rows, g_rows = q[rows, :], g[rows, :]
        dots = jnp.zeros((8, block), F32)
        for j in range(i + 1):
            cols = pl.ds(j * block, block)
            dp = dot(v[cols, :], g_rows, ROWS_BY_ROWS)
            slopes[cols, :] = dp
            dots = dots + fold(probs[place(i, j)] * dp, jnp.sum)
        row_dots = jnp.sum(dots, axis=0, keepdims=True)
        query_total = jnp.zeros((width, block), F32)
        for j in range(i + 1):
            cols = pl.ds(j * block, block)
            ds = (probs[place(i, j)] * (slopes[cols, :] - row_dots)).astype(BF16)
            dk = dot(ds, q_rows, PLAIN)
            if i == blocks - 1:
                key_total[cols, :] = dk
            else:
                key_total[cols, :] += dk
            query_total = query_total + dot(k_turned[:, cols], ds, PLAIN)
        put(i, (query_total.T * scaling).astype(BF16), (key_total[rows, :] * scaling).astype(BF16))


def kernel(
    sections, groups, heads, tokens, block, slots,
    codes, store, slope, out,
    store_in0, store_in1, store_in2, slope_in, far_out, own_out, grad_out,
    far, own, grad, sel, done, probs, slopes, key_total, value_total, k_turned,
    load_sem, far_send, far_recv, own_send, own_recv, grad_send, grad_recv, out_send, out_recv,
):
    s = lax.axis_index("section")
    t = lax.axis_index("tp")
    mirror = sections - 1 - s
    length = groups * tokens
    triple = store.shape[2]
    mine = pl.ds(pl.multiple_of(t * tokens, tokens), tokens)
    step = 16
    store_in = (store_in0, store_in1, store_in2)

    def load(w):
        return pltpu.make_async_copy(store.at[:, :, w], store_in[w], load_sem.at[w])

    def load_slope():
        return pltpu.make_async_copy(slope, slope_in, load_sem.at[triple])

    for w in range(triple):
        load(w).start()
    load_slope().start()

    barrier = pltpu.get_barrier_semaphore()

    def greet(i, _):
        peer = lax.bitwise_xor(t, i)
        pl.semaphore_signal(barrier, inc=1, device_id=(mirror, peer), device_id_type=MESH)

        @pl.when(i > 0)
        def _():
            pl.semaphore_signal(barrier, inc=1, device_id=(s, peer), device_id_type=MESH)

        return 0

    lax.fori_loop(0, groups, greet, 0)
    home = codes[s]
    away = codes[mirror]
    own_slot = jnp.clip(home, 0, slots - 1)
    far_slot = jnp.clip(away - slots, 0, slots - 1)
    take_far = home >= slots

    def by_head(slot, w, to):
        def f(n, _):
            rows = pl.ds(pl.multiple_of(n * step, step), step)
            to[w, :, rows, :] = jnp.swapaxes(store_in[w][slot, rows], 0, 1)
            return 0

        lax.fori_loop(0, tokens // step, f, 0)

    def each_peer(first, f):
        def g(n, _):
            f(lax.bitwise_xor(t, chips_first(n)))
            return 0

        lax.fori_loop(first, groups, g, 0)

    def send_far(hd, w, classes=False):
        def f(peer):
            pltpu.make_async_remote_copy(
                src_ref=far_out.at[w, peer * heads + hd], dst_ref=far.at[hd, w, mine, :],
                send_sem=far_send.at[hd, w], recv_sem=far_recv.at[hd, w],
                device_id=(mirror, peer), device_id_type=MESH,
            ).start()

        if classes:
            def g(n, _):
                order = n // 4
                f(order % 2 * 8 + lax.bitwise_xor(t // 2 % 4, n % 4) * 2 + order // 2)
                return 0

            lax.fori_loop(0, groups, g, 0)
        else:
            each_peer(0, f)

    def far_sent(hd, w):
        some = pl.ds(0, groups)
        pltpu.make_async_copy(far_out.at[w, some], far_out.at[w, some], far_send.at[hd, w]).wait()

    def far_here(hd, w):
        pltpu.make_async_copy(far.at[hd, w], far.at[hd, w], far_recv.at[hd, w]).wait()

    def send_own(hd):
        pltpu.make_async_copy(own_out.at[:, t * heads + hd], own.at[hd, :, mine, :], own_recv.at[hd]).start()
        pltpu.make_async_copy(grad_out.at[t * heads + hd], grad.at[hd, mine, :], grad_recv.at[hd]).start()

        def f(peer):
            pltpu.make_async_remote_copy(
                src_ref=own_out.at[:, peer * heads + hd], dst_ref=own.at[hd, :, mine, :],
                send_sem=own_send, recv_sem=own_recv.at[hd],
                device_id=(s, peer), device_id_type=MESH,
            ).start()
            pltpu.make_async_remote_copy(
                src_ref=grad_out.at[peer * heads + hd], dst_ref=grad.at[hd, mine, :],
                send_sem=grad_send, recv_sem=grad_recv.at[hd],
                device_id=(s, peer), device_id_type=MESH,
            ).start()

        each_peer(1, f)

    late = pl.ds(triple - 1, 1)
    early = pl.ds(0, triple - 1)
    last = triple - 1

    def slope_by_head(n, _):
        rows = pl.ds(pl.multiple_of(n * step, step), step)
        grad_out[:, rows, :] = jnp.swapaxes(slope_in[rows], 0, 1)
        return 0

    load(1).wait()
    by_head(far_slot, 1, far_out)
    pl.semaphore_wait(barrier, 2 * groups - 1)
    send_far(0, 1)
    load(0).wait()
    by_head(far_slot, 0, far_out)
    send_far(0, 0)
    load_slope().wait()
    lax.fori_loop(0, tokens // step, slope_by_head, 0)
    load(last).wait()
    for w in range(triple):
        by_head(own_slot, w, own_out)
    send_own(0)
    by_head(far_slot, last, far_out)
    send_far(0, last)
    for hd in range(1, heads):
        send_own(hd)
    far_sent(0, 1)
    send_far(1, 1)
    far_sent(0, 0)
    send_far(1, 0)

    def one_head(hd, _):
        pltpu.make_async_copy(own.at[hd], own.at[hd], own_recv.at[hd]).wait()
        pltpu.make_async_copy(grad.at[hd], grad.at[hd], grad_recv.at[hd]).wait()
        far_here(hd, 1)
        far_here(hd, 0)

        def choose(ws):
            def f(n, _):
                rows = pl.ds(pl.multiple_of(n * block, block), block)
                sel[ws, rows, :] = jnp.where(take_far, far[hd, ws, rows, :], own[hd, ws, rows, :])
                return 0

            lax.fori_loop(0, length // block, f, 0)

        per = block // tokens

        def put_value(i, dv):
            for n in range(per):
                done[hd, i * per + n, 2] = dv[n * tokens:(n + 1) * tokens]

        def put_query_key(i, dq, dk):
            for n in range(per):
                done[hd, i * per + n, 0] = dq[n * tokens:(n + 1) * tokens]
                done[hd, i * per + n, 1] = dk[n * tokens:(n + 1) * tokens]

        def give(peer, ws):
            @pl.when(peer == t)
            def _():
                pltpu.make_async_copy(done.at[hd, peer, ws], out.at[t, hd, ws], out_recv).start()

            @pl.when(peer != t)
            def _():
                pltpu.make_async_remote_copy(
                    src_ref=done.at[hd, peer, ws], dst_ref=out.at[t, hd, ws],
                    send_sem=out_send, recv_sem=out_recv,
                    device_id=(s, peer), device_id_type=MESH,
                ).start()

        choose(early)
        q, k, v, g = sel.at[0], sel.at[1], sel.at[2], grad.at[hd]
        k_turned[...] = k[...].T
        softmax_and_value_grad(q, k, g, probs, value_total, put_value, length, block)
        each_peer(0, lambda peer: give(peer, late))

        @pl.when(hd + 1 < heads)
        def _():
            far_sent(hd, last)
            send_far(hd + 1, last, classes=True)

        far_here(hd, last)
        choose(late)
        blocks = length // block
        half = groups // 2
        for part in (1, 0):
            which = reversed(range(part * blocks // 2, (part + 1) * blocks // 2))
            query_and_key_grad(
                q, k, v, g, probs, slopes, key_total, k_turned, put_query_key, length, block, which
            )

            def f(n, _):
                give(part * half + lax.rem(lax.bitwise_xor(t, chips_first(n)), half), early)
                return 0

            lax.fori_loop(0, half, f, 0)
        return 0

    lax.fori_loop(0, heads, one_head, 0)

    for w in range(triple):
        far_sent(heads - 1, w)
    sent = pl.ds(0, (groups - 1) * heads)
    pltpu.make_async_copy(own_out.at[:, sent], own_out.at[:, sent], own_send).wait()
    pltpu.make_async_copy(grad_out.at[sent], grad_out.at[sent], grad_send).wait()
    rest = pl.ds(1, groups - 1)
    pltpu.make_async_copy(out.at[rest], out.at[rest], out_send).wait()
    pltpu.make_async_copy(out, out, out_recv).wait()


def by_token(parts, whole, came, turned, load_sem, store_sem):
    groups, heads, triple, tokens, width = parts.shape
    step = 16
    loads = [pltpu.make_async_copy(parts.at[:, :, w], came.at[w], load_sem.at[w]) for w in range(triple)]
    stores = [pltpu.make_async_copy(turned.at[w], whole.at[:, w], store_sem.at[w]) for w in range(triple)]
    for load in loads:
        load.start()
    for w in range(triple):
        loads[w].wait()
        for n in range(tokens // step):
            rows = pl.ds(n * step, step)
            piece = came[w, :, :, rows, :].reshape(groups * heads, step, width)
            turned[w, rows] = jnp.swapaxes(piece, 0, 1)
        stores[w].start()
    for store in stores:
        store.wait()


def solution(mesh):
    sections, groups = mesh.shape["section"], mesh.shape["tp"]

    def local(saved_caches, keeper_code, result_slope):
        slots, tokens, triple, head_count, width = saved_caches.shape[1:]
        heads = head_count // groups
        length = groups * tokens
        block = 256
        blocks = length // block
        anywhere = pl.BlockSpec(memory_space=pl.ANY)
        vmem = pltpu.VMEM
        sem = pltpu.SemaphoreType.DMA
        out = pl.pallas_call(
            functools.partial(kernel, sections, groups, heads, tokens, block, slots),
            out_shape=jax.ShapeDtypeStruct((groups, heads, triple, tokens, width), BF16),
            in_specs=[pl.BlockSpec(memory_space=pltpu.SMEM), anywhere, anywhere],
            out_specs=anywhere,
            scratch_shapes=[
                *[vmem((slots, tokens, head_count, width), BF16)] * triple,
                vmem((tokens, head_count, width), BF16),
                vmem((triple, head_count, tokens, width), BF16),
                vmem((triple, head_count, tokens, width), BF16),
                vmem((head_count, tokens, width), BF16),
                vmem((heads, triple, length, width), BF16),
                vmem((heads, triple, length, width), BF16),
                vmem((heads, length, width), BF16),
                vmem((triple, length, width), BF16),
                vmem((heads, groups, triple, tokens, width), BF16),
                vmem((place(blocks, 0), block, block), F32),
                vmem((length, block), F32),
                vmem((length, width), F32),
                vmem((length, width), F32),
                vmem((width, length), BF16),
                sem((triple + 1,)),
                sem((heads, triple)), sem((heads, triple)), sem, sem((heads,)), sem, sem((heads,)), sem, sem,
            ],
            compiler_params=pltpu.CompilerParams(
                collective_id=0, has_side_effects=True, vmem_limit_bytes=56 * 2**20
            ),
        )(keeper_code, saved_caches[0], result_slope[0])
        whole = pl.pallas_call(
            by_token,
            out_shape=jax.ShapeDtypeStruct((tokens, triple, head_count, width), BF16),
            in_specs=[anywhere],
            out_specs=anywhere,
            scratch_shapes=[
                vmem((triple, groups, heads, tokens, width), BF16),
                vmem((triple, tokens, head_count, width), BF16),
                sem((triple,)), sem((triple,)),
            ],
            compiler_params=pltpu.CompilerParams(vmem_limit_bytes=56 * 2**20),
        )(out)
        return whole[None]

    return jax.shard_map(
        local,
        mesh=mesh,
        in_specs=(P("section", None, "tp", None, None, None), P(), P("section", "tp", None, None)),
        out_specs=P("section", "tp", None, None, None),
        check_vma=False,
    )
```

```python
import functools

import jax
import jax.numpy as jnp
from jax import lax
from jax.experimental import pallas as pl
from jax.experimental.pallas import tpu as pltpu
from jax.sharding import PartitionSpec as P

MESH = pl.DeviceIdType.MESH
F32 = jnp.float32
BF16 = jnp.bfloat16
LOG2E = 1.4426950408889634
ROWS_BY_ROWS = (((1,), (1,)), ((), ()))
PLAIN = (((1,), (0,)), ((), ()))


def dot(a, b, dims):
    return lax.dot_general(a, b, dims, preferred_element_type=F32)


def fold(x, op):
    return op(x.reshape(x.shape[0] // 8, 8, x.shape[1]), axis=0)


def chips_first(n):
    return n % 4 * 2 + n // 4 % 2 + n // 8 * 8


def place(i, j):
    return i * (i + 1) // 2 + j


def softmax_and_value_grad(q, k, g, probs, value_total, put, length, block):
    exponent = q.shape[-1] ** (-0.5) * LOG2E
    blocks = length // block
    key_ids = lax.broadcasted_iota(jnp.int32, (block, block), 0)
    query_ids = lax.broadcasted_iota(jnp.int32, (block, block), 1)
    causal = key_ids <= query_ids
    for i in reversed(range(blocks)):
        rows = pl.ds(i * block, block)
        q_rows, g_rows = q[rows, :], g[rows, :]
        peak = jnp.full((8, block), -3.0e38, F32)
        for j in range(i + 1):
            s = dot(k[pl.ds(j * block, block), :], q_rows, ROWS_BY_ROWS)
            if j == i:
                s = jnp.where(causal, s, F32(-1e30))
            probs[place(i, j)] = s
            peak = jnp.maximum(peak, fold(s, jnp.max))
        peak = jnp.max(peak, axis=0, keepdims=True)
        total = jnp.zeros((8, block), F32)
        for j in range(i + 1):
            e = jnp.exp2((probs[place(i, j)] - peak) * exponent)
            probs[place(i, j)] = e
            total = total + fold(e, jnp.sum)
        inverse = 1.0 / jnp.sum(total, axis=0, keepdims=True)
        for j in range(i + 1):
            cols = pl.ds(j * block, block)
            p = probs[place(i, j)] * inverse
            probs[place(i, j)] = p
            dv = dot(p.astype(BF16), g_rows, PLAIN)
            if i == blocks - 1:
                value_total[cols, :] = dv
            else:
                value_total[cols, :] += dv
        put(i, value_total[rows, :].astype(BF16))


def query_and_key_grad(q, k, v, g, probs, slopes, key_total, k_turned, put, length, block):
    width = q.shape[-1]
    scaling = width ** (-0.5)
    blocks = length // block

    def ahead(i):
        g_rows = g[pl.ds(i * block, block), :]
        dots = jnp.zeros((8, block), F32)
        for j in range(i + 1):
            cols = pl.ds(j * block, block)
            dp = dot(v[cols, :], g_rows, ROWS_BY_ROWS)
            slopes[i % 2, cols, :] = dp
            dots = dots + fold(probs[place(i, j)] * dp, jnp.sum)
        return jnp.sum(dots, axis=0, keepdims=True)

    next_dots = ahead(blocks - 1)
    for i in reversed(range(blocks)):
        rows = pl.ds(i * block, block)
        q_rows = q[rows, :]
        row_dots = next_dots
        if i > 0:
            next_dots = ahead(i - 1)
        query_total = jnp.zeros((width, block), F32)
        for j in range(i + 1):
            cols = pl.ds(j * block, block)
            ds = (probs[place(i, j)] * (slopes[i % 2, cols, :] - row_dots)).astype(BF16)
            dk = dot(ds, q_rows, PLAIN)
            if i == blocks - 1:
                key_total[cols, :] = dk
            else:
                key_total[cols, :] += dk
            query_total = query_total + dot(k_turned[:, cols], ds, PLAIN)
        put(i, (query_total.T * scaling).astype(BF16), (key_total[rows, :] * scaling).astype(BF16))


def kernel(
    sections, groups, heads, tokens, block, slots,
    codes, store, slope, out,
    store_in0, store_in1, store_in2, slope_in, far_out, own_out, grad_out,
    far, own, grad, sel, done, probs, slopes, key_total, value_total, k_turned,
    load_sem, far_send, far_recv, own_send, own_recv, grad_send, grad_recv, out_send, out_recv,
):
    s = lax.axis_index("section")
    t = lax.axis_index("tp")
    mirror = sections - 1 - s
    length = groups * tokens
    triple = store.shape[2]
    mine = pl.ds(pl.multiple_of(t * tokens, tokens), tokens)
    step = 16
    store_in = (store_in0, store_in1, store_in2)

    def load(w):
        return pltpu.make_async_copy(store.at[:, :, w], store_in[w], load_sem.at[w])

    def load_slope():
        return pltpu.make_async_copy(slope, slope_in, load_sem.at[triple])

    for w in (1, 0, 2):
        load(w).start()
    load_slope().start()

    barrier = pltpu.get_barrier_semaphore()

    def greet(i, _):
        peer = lax.bitwise_xor(t, i)
        pl.semaphore_signal(barrier, inc=1, device_id=(mirror, peer), device_id_type=MESH)

        @pl.when(i > 0)
        def _():
            pl.semaphore_signal(barrier, inc=1, device_id=(s, peer), device_id_type=MESH)

        return 0

    lax.fori_loop(0, groups, greet, 0)
    home = codes[s]
    away = codes[mirror]
    own_slot = jnp.clip(home, 0, slots - 1)
    far_slot = jnp.clip(away - slots, 0, slots - 1)
    take_far = home >= slots

    def by_head(slot, w, to):
        def f(n, _):
            rows = pl.ds(pl.multiple_of(n * step, step), step)
            to[w, :, rows, :] = jnp.swapaxes(store_in[w][slot, rows], 0, 1)
            return 0

        lax.fori_loop(0, tokens // step, f, 0)

    def each_peer(first, f):
        def g(n, _):
            f(lax.bitwise_xor(t, chips_first(n)))
            return 0

        lax.fori_loop(first, groups, g, 0)

    def send_far(hd, w, classes=False):
        def f(peer):
            pltpu.make_async_remote_copy(
                src_ref=far_out.at[w, peer * heads + hd], dst_ref=far.at[hd, w, mine, :],
                send_sem=far_send.at[hd, w], recv_sem=far_recv.at[hd, w],
                device_id=(mirror, peer), device_id_type=MESH,
            ).start()

        if classes:
            def g(n, _):
                order = n // 4
                f(order % 2 * 8 + lax.bitwise_xor(t // 2 % 4, n % 4) * 2 + order // 2)
                return 0

            lax.fori_loop(0, groups, g, 0)
        else:
            each_peer(0, f)

    def far_sent(hd, w):
        some = pl.ds(0, groups)
        pltpu.make_async_copy(far_out.at[w, some], far_out.at[w, some], far_send.at[hd, w]).wait()

    def far_here(hd, w):
        pltpu.make_async_copy(far.at[hd, w], far.at[hd, w], far_recv.at[hd, w]).wait()

    def send_own(hd):
        pltpu.make_async_copy(own_out.at[:, t * heads + hd], own.at[hd, :, mine, :], own_recv.at[hd]).start()
        pltpu.make_async_copy(grad_out.at[t * heads + hd], grad.at[hd, mine, :], grad_recv.at[hd]).start()

        def f(peer):
            pltpu.make_async_remote_copy(
                src_ref=own_out.at[:, peer * heads + hd], dst_ref=own.at[hd, :, mine, :],
                send_sem=own_send, recv_sem=own_recv.at[hd],
                device_id=(s, peer), device_id_type=MESH,
            ).start()
            pltpu.make_async_remote_copy(
                src_ref=grad_out.at[peer * heads + hd], dst_ref=grad.at[hd, mine, :],
                send_sem=grad_send, recv_sem=grad_recv.at[hd],
                device_id=(s, peer), device_id_type=MESH,
            ).start()

        each_peer(1, f)

    late = pl.ds(triple - 1, 1)
    early = pl.ds(0, triple - 1)
    last = triple - 1

    def slope_by_head(n, _):
        rows = pl.ds(pl.multiple_of(n * step, step), step)
        grad_out[:, rows, :] = jnp.swapaxes(slope_in[rows], 0, 1)
        return 0

    load(1).wait()
    by_head(far_slot, 1, far_out)
    load(0).wait()
    by_head(far_slot, 0, far_out)
    load(last).wait()
    load_slope().wait()
    for w in range(triple):
        by_head(own_slot, w, own_out)
    lax.fori_loop(0, tokens // step, slope_by_head, 0)
    pl.semaphore_wait(barrier, 2 * groups - 1)
    send_far(0, 1)
    send_own(0)
    send_far(0, 0)
    by_head(far_slot, last, far_out)
    send_far(0, last)
    for hd in range(1, heads):
        send_own(hd)
    far_sent(0, 1)
    send_far(1, 1)
    far_sent(0, 0)
    send_far(1, 0)

    def one_head(hd, _):
        pltpu.make_async_copy(own.at[hd], own.at[hd], own_recv.at[hd]).wait()
        pltpu.make_async_copy(grad.at[hd], grad.at[hd], grad_recv.at[hd]).wait()
        far_here(hd, 1)
        far_here(hd, 0)

        def choose(ws):
            def f(n, _):
                rows = pl.ds(pl.multiple_of(n * block, block), block)
                sel[ws, rows, :] = jnp.where(take_far, far[hd, ws, rows, :], own[hd, ws, rows, :])
                return 0

            lax.fori_loop(0, length // block, f, 0)

        per = block // tokens

        def put_value(i, dv):
            for n in range(per):
                done[hd, i * per + n, 2] = dv[n * tokens:(n + 1) * tokens]

        def give(peer, ws):
            @pl.when(peer == t)
            def _():
                pltpu.make_async_copy(done.at[hd, peer, ws], out.at[t, hd, ws], out_recv).start()

            @pl.when(peer != t)
            def _():
                pltpu.make_async_remote_copy(
                    src_ref=done.at[hd, peer, ws], dst_ref=out.at[t, hd, ws],
                    send_sem=out_send, recv_sem=out_recv,
                    device_id=(s, peer), device_id_type=MESH,
                ).start()

        choose(early)
        q, k, v, g = sel.at[0], sel.at[1], sel.at[2], grad.at[hd]
        k_turned[...] = k[...].T
        softmax_and_value_grad(q, k, g, probs, value_total, put_value, length, block)
        each_peer(0, lambda peer: give(peer, late))

        @pl.when(hd + 1 < heads)
        def _():
            far_sent(hd, last)
            send_far(hd + 1, last, classes=True)

        far_here(hd, last)
        choose(late)
        half = groups // 2

        def put_query_key(i, dq, dk):
            for n in range(per):
                done[hd, i * per + n, 0] = dq[n * tokens:(n + 1) * tokens]
                done[hd, i * per + n, 1] = dk[n * tokens:(n + 1) * tokens]
            if i * per % half == 0:

                def f(n, _):
                    give(i * per + lax.rem(lax.bitwise_xor(t, chips_first(n)), half), early)
                    return 0

                lax.fori_loop(0, half, f, 0)

        query_and_key_grad(q, k, v, g, probs, slopes, key_total, k_turned, put_query_key, length, block)
        return 0

    lax.fori_loop(0, heads, one_head, 0)

    for w in range(triple):
        far_sent(heads - 1, w)
    sent = pl.ds(0, (groups - 1) * heads)
    pltpu.make_async_copy(own_out.at[:, sent], own_out.at[:, sent], own_send).wait()
    pltpu.make_async_copy(grad_out.at[sent], grad_out.at[sent], grad_send).wait()
    rest = pl.ds(1, groups - 1)
    pltpu.make_async_copy(out.at[rest], out.at[rest], out_send).wait()
    pltpu.make_async_copy(out, out, out_recv).wait()


def by_token(parts, whole, came, turned, load_sem, store_sem):
    groups, heads, triple, tokens, width = parts.shape
    step = 16
    chunk = tokens // 4
    chunks = [(c, w) for c in range(tokens // chunk) for w in range(triple)]
    loads, stores = [], []
    for at, (c, w) in enumerate(chunks):
        rows = pl.ds(c * chunk, chunk)
        loads.append(pltpu.make_async_copy(parts.at[:, :, w, rows], came.at[c, w], load_sem.at[at]))
        stores.append(pltpu.make_async_copy(turned.at[c, w], whole.at[rows, w], store_sem.at[at]))
    for load in loads:
        load.start()
    for at, (c, w) in enumerate(chunks):
        loads[at].wait()
        for n in range(chunk // step):
            rows = pl.ds(n * step, step)
            piece = came[c, w, :, :, rows, :].reshape(groups * heads, step, width)
            turned[c, w, rows] = jnp.swapaxes(piece, 0, 1)
        stores[at].start()
    for store in stores:
        store.wait()


def solution(mesh):
    sections, groups = mesh.shape["section"], mesh.shape["tp"]

    def local(saved_caches, keeper_code, result_slope):
        slots, tokens, triple, head_count, width = saved_caches.shape[1:]
        heads = head_count // groups
        length = groups * tokens
        block = 256
        blocks = length // block
        anywhere = pl.BlockSpec(memory_space=pl.ANY)
        vmem = pltpu.VMEM
        sem = pltpu.SemaphoreType.DMA
        out = pl.pallas_call(
            functools.partial(kernel, sections, groups, heads, tokens, block, slots),
            out_shape=jax.ShapeDtypeStruct((groups, heads, triple, tokens, width), BF16),
            in_specs=[pl.BlockSpec(memory_space=pltpu.SMEM), anywhere, anywhere],
            out_specs=anywhere,
            scratch_shapes=[
                *[vmem((slots, tokens, head_count, width), BF16)] * triple,
                vmem((tokens, head_count, width), BF16),
                vmem((triple, head_count, tokens, width), BF16),
                vmem((triple, head_count, tokens, width), BF16),
                vmem((head_count, tokens, width), BF16),
                vmem((heads, triple, length, width), BF16),
                vmem((heads, triple, length, width), BF16),
                vmem((heads, length, width), BF16),
                vmem((triple, length, width), BF16),
                vmem((heads, groups, triple, tokens, width), BF16),
                vmem((place(blocks, 0), block, block), F32),
                vmem((2, length, block), F32),
                vmem((length, width), F32),
                vmem((length, width), F32),
                vmem((width, length), BF16),
                sem((triple + 1,)),
                sem((heads, triple)), sem((heads, triple)), sem, sem((heads,)), sem, sem((heads,)), sem, sem,
            ],
            compiler_params=pltpu.CompilerParams(
                collective_id=0, has_side_effects=True, vmem_limit_bytes=56 * 2**20
            ),
        )(keeper_code, saved_caches[0], result_slope[0])
        whole = pl.pallas_call(
            by_token,
            out_shape=jax.ShapeDtypeStruct((tokens, triple, head_count, width), BF16),
            in_specs=[anywhere],
            out_specs=anywhere,
            scratch_shapes=[
                vmem((4, triple, groups, heads, tokens // 4, width), BF16),
                vmem((4, triple, tokens // 4, head_count, width), BF16),
                sem((4 * triple,)), sem((4 * triple,)),
            ],
            compiler_params=pltpu.CompilerParams(vmem_limit_bytes=56 * 2**20),
        )(out)
        return whole[None]

    return jax.shard_map(
        local,
        mesh=mesh,
        in_specs=(P("section", None, "tp", None, None, None), P(), P("section", "tp", None, None)),
        out_specs=P("section", "tp", None, None, None),
        check_vma=False,
    )
```

```python
import functools

import jax
import jax.numpy as jnp
from jax import lax
from jax.experimental import pallas as pl
from jax.experimental.pallas import tpu as pltpu
from jax.sharding import PartitionSpec as P

MESH = pl.DeviceIdType.MESH
F32 = jnp.float32
BF16 = jnp.bfloat16
LOG2E = 1.4426950408889634
ROWS_BY_ROWS = (((1,), (1,)), ((), ()))
PLAIN = (((1,), (0,)), ((), ()))


def dot(a, b, dims):
    return lax.dot_general(a, b, dims, preferred_element_type=F32)


def fold(x, op):
    return op(x.reshape(x.shape[0] // 8, 8, x.shape[1]), axis=0)


def chips_first(n):
    return n % 4 * 2 + n // 4 % 2 + n // 8 * 8


def place(i, j):
    return i * (i + 1) // 2 + j


def softmax_and_value_grad(q, k, g, probs, value_total, put, length, block):
    exponent = q.shape[-1] ** (-0.5) * LOG2E
    blocks = length // block
    key_ids = lax.broadcasted_iota(jnp.int32, (block, block), 0)
    query_ids = lax.broadcasted_iota(jnp.int32, (block, block), 1)
    causal = key_ids <= query_ids
    for i in reversed(range(blocks)):
        rows = pl.ds(i * block, block)
        q_rows, g_rows = q[rows, :], g[rows, :]
        peak = jnp.full((8, block), -3.0e38, F32)
        for j in range(i + 1):
            s = dot(k[pl.ds(j * block, block), :], q_rows, ROWS_BY_ROWS)
            if j == i:
                s = jnp.where(causal, s, F32(-1e30))
            probs[place(i, j)] = s
            peak = jnp.maximum(peak, fold(s, jnp.max))
        peak = jnp.max(peak, axis=0, keepdims=True)
        total = jnp.zeros((8, block), F32)
        for j in range(i + 1):
            e = jnp.exp2((probs[place(i, j)] - peak) * exponent)
            probs[place(i, j)] = e
            total = total + fold(e, jnp.sum)
        inverse = 1.0 / jnp.sum(total, axis=0, keepdims=True)
        for j in range(i + 1):
            cols = pl.ds(j * block, block)
            p = probs[place(i, j)] * inverse
            probs[place(i, j)] = p
            dv = dot(p.astype(BF16), g_rows, PLAIN)
            if i == blocks - 1:
                value_total[cols, :] = dv
            else:
                value_total[cols, :] += dv
        put(i, value_total[rows, :].astype(BF16))


def query_and_key_grad(q, k, v, g, probs, slopes, key_total, k_turned, put, length, block):
    width = q.shape[-1]
    scaling = width ** (-0.5)
    blocks = length // block

    def ahead(i):
        g_rows = g[pl.ds(i * block, block), :]
        dots = jnp.zeros((8, block), F32)
        for j in range(i + 1):
            cols = pl.ds(j * block, block)
            dp = dot(v[cols, :], g_rows, ROWS_BY_ROWS)
            slopes[i % 2, cols, :] = dp
            dots = dots + fold(probs[place(i, j)] * dp, jnp.sum)
        return jnp.sum(dots, axis=0, keepdims=True)

    next_dots = ahead(blocks - 1)
    for i in reversed(range(blocks)):
        rows = pl.ds(i * block, block)
        q_rows = q[rows, :]
        row_dots = next_dots
        if i > 0:
            next_dots = ahead(i - 1)
        query_total = jnp.zeros((width, block), F32)
        for j in range(i + 1):
            cols = pl.ds(j * block, block)
            ds = (probs[place(i, j)] * (slopes[i % 2, cols, :] - row_dots)).astype(BF16)
            dk = dot(ds, q_rows, PLAIN)
            if i == blocks - 1:
                key_total[cols, :] = dk
            else:
                key_total[cols, :] += dk
            query_total = query_total + dot(k_turned[:, cols], ds, PLAIN)
        put(i, (query_total.T * scaling).astype(BF16), (key_total[rows, :] * scaling).astype(BF16))


def kernel(
    sections, groups, heads, tokens, block, slots,
    codes, store, slope, out,
    store_in0, store_in1, store_in2, slope_in, far_out, own_out, grad_out,
    far, own, grad, sel, done, probs, slopes, key_total, value_total, k_turned,
    ready, load_sem, far_send, far_recv, own_send, own_recv, grad_send, grad_recv, out_send, out_recv,
):
    s = lax.axis_index("section")
    t = lax.axis_index("tp")
    mirror = sections - 1 - s
    length = groups * tokens
    triple = store.shape[2]
    mine = pl.ds(pl.multiple_of(t * tokens, tokens), tokens)
    step = 16
    store_in = (store_in0, store_in1, store_in2)

    def load(w):
        return pltpu.make_async_copy(store.at[:, :, w], store_in[w], load_sem.at[w])

    def load_slope():
        return pltpu.make_async_copy(slope, slope_in, load_sem.at[triple])

    for w in (1, 0, 2):
        load(w).start()
    load_slope().start()

    barrier = pltpu.get_barrier_semaphore()

    first = lax.rem(s, 4) < 2
    second = lax.rem(s, 4) >= 2

    def greet(i, _):
        peer = lax.bitwise_xor(t, i)

        @pl.when(i > 0)
        def _():
            pl.semaphore_signal(barrier, inc=1, device_id=(s, peer), device_id_type=MESH)

        @pl.when(first)
        def _():
            pl.semaphore_signal(barrier, inc=1, device_id=(mirror, peer), device_id_type=MESH)

        return 0

    lax.fori_loop(0, groups, greet, 0)

    def answer(i, _):
        pl.semaphore_signal(
            ready, inc=1, device_id=(mirror, lax.bitwise_xor(t, i)), device_id_type=MESH
        )
        return 0

    home = codes[s]
    away = codes[mirror]
    own_slot = jnp.clip(home, 0, slots - 1)
    far_slot = jnp.clip(away - slots, 0, slots - 1)
    take_far = home >= slots

    def by_head(slot, w, to):
        def f(n, _):
            rows = pl.ds(pl.multiple_of(n * step, step), step)
            to[w, :, rows, :] = jnp.swapaxes(store_in[w][slot, rows], 0, 1)
            return 0

        lax.fori_loop(0, tokens // step, f, 0)

    def each_peer(first, f):
        def g(n, _):
            f(lax.bitwise_xor(t, chips_first(n)))
            return 0

        lax.fori_loop(first, groups, g, 0)

    def send_far(hd, w, classes=False):
        def f(peer):
            pltpu.make_async_remote_copy(
                src_ref=far_out.at[w, peer * heads + hd], dst_ref=far.at[hd, w, mine, :],
                send_sem=far_send.at[hd, w], recv_sem=far_recv.at[hd, w],
                device_id=(mirror, peer), device_id_type=MESH,
            ).start()

        if classes:
            def g(n, _):
                order = n // 4
                f(order % 2 * 8 + lax.bitwise_xor(t // 2 % 4, n % 4) * 2 + order // 2)
                return 0

            lax.fori_loop(0, groups, g, 0)
        else:
            each_peer(0, f)

    def far_sent(hd, w):
        some = pl.ds(0, groups)
        pltpu.make_async_copy(far_out.at[w, some], far_out.at[w, some], far_send.at[hd, w]).wait()

    def far_here(hd, w):
        pltpu.make_async_copy(far.at[hd, w], far.at[hd, w], far_recv.at[hd, w]).wait()

    def send_own(hd):
        pltpu.make_async_copy(own_out.at[:, t * heads + hd], own.at[hd, :, mine, :], own_recv.at[hd]).start()
        pltpu.make_async_copy(grad_out.at[t * heads + hd], grad.at[hd, mine, :], grad_recv.at[hd]).start()

        def f(peer):
            pltpu.make_async_remote_copy(
                src_ref=own_out.at[:, peer * heads + hd], dst_ref=own.at[hd, :, mine, :],
                send_sem=own_send, recv_sem=own_recv.at[hd],
                device_id=(s, peer), device_id_type=MESH,
            ).start()
            pltpu.make_async_remote_copy(
                src_ref=grad_out.at[peer * heads + hd], dst_ref=grad.at[hd, mine, :],
                send_sem=grad_send, recv_sem=grad_recv.at[hd],
                device_id=(s, peer), device_id_type=MESH,
            ).start()

        each_peer(1, f)

    late = pl.ds(triple - 1, 1)
    early = pl.ds(0, triple - 1)
    last = triple - 1

    def slope_by_head(n, _):
        rows = pl.ds(pl.multiple_of(n * step, step), step)
        grad_out[:, rows, :] = jnp.swapaxes(slope_in[rows], 0, 1)
        return 0

    load(1).wait()
    by_head(far_slot, 1, far_out)

    @pl.when(second)
    def _():
        pl.semaphore_wait(barrier, 2 * groups - 1)
        lax.fori_loop(0, groups, answer, 0)
        send_far(0, 1)

    load(0).wait()
    load(last).wait()
    load_slope().wait()
    for w in range(triple):
        by_head(own_slot, w, own_out)
    lax.fori_loop(0, tokens // step, slope_by_head, 0)

    @pl.when(first)
    def _():
        pl.semaphore_wait(barrier, groups - 1)

    send_own(0)
    by_head(far_slot, 0, far_out)

    @pl.when(second)
    def _():
        send_far(0, 0)

    by_head(far_slot, last, far_out)

    @pl.when(first)
    def _():
        for hd in range(1, heads):
            send_own(hd)
        pl.semaphore_wait(ready, groups)
        send_far(0, 1)
        send_far(0, 0)

    send_far(0, last)

    @pl.when(second)
    def _():
        for hd in range(1, heads):
            send_own(hd)

    far_sent(0, 1)
    send_far(1, 1)
    far_sent(0, 0)
    send_far(1, 0)

    def one_head(hd, _):
        pltpu.make_async_copy(own.at[hd], own.at[hd], own_recv.at[hd]).wait()
        pltpu.make_async_copy(grad.at[hd], grad.at[hd], grad_recv.at[hd]).wait()
        far_here(hd, 1)
        far_here(hd, 0)

        def choose(ws):
            def f(n, _):
                rows = pl.ds(pl.multiple_of(n * block, block), block)
                sel[ws, rows, :] = jnp.where(take_far, far[hd, ws, rows, :], own[hd, ws, rows, :])
                return 0

            lax.fori_loop(0, length // block, f, 0)

        per = block // tokens

        def put_value(i, dv):
            for n in range(per):
                done[hd, i * per + n, 2] = dv[n * tokens:(n + 1) * tokens]

        def give(peer, ws):
            @pl.when(peer == t)
            def _():
                pltpu.make_async_copy(done.at[hd, peer, ws], out.at[t, hd, ws], out_recv).start()

            @pl.when(peer != t)
            def _():
                pltpu.make_async_remote_copy(
                    src_ref=done.at[hd, peer, ws], dst_ref=out.at[t, hd, ws],
                    send_sem=out_send, recv_sem=out_recv,
                    device_id=(s, peer), device_id_type=MESH,
                ).start()

        choose(early)
        q, k, v, g = sel.at[0], sel.at[1], sel.at[2], grad.at[hd]
        k_turned[...] = k[...].T
        softmax_and_value_grad(q, k, g, probs, value_total, put_value, length, block)
        each_peer(0, lambda peer: give(peer, late))

        @pl.when(hd + 1 < heads)
        def _():
            far_sent(hd, last)
            send_far(hd + 1, last, classes=True)

        far_here(hd, last)
        choose(late)
        half = groups // 2

        def put_query_key(i, dq, dk):
            for n in range(per):
                done[hd, i * per + n, 0] = dq[n * tokens:(n + 1) * tokens]
                done[hd, i * per + n, 1] = dk[n * tokens:(n + 1) * tokens]
            if i * per % half == 0:

                def f(n, _):
                    give(i * per + lax.rem(lax.bitwise_xor(t, chips_first(n)), half), early)
                    return 0

                lax.fori_loop(0, half, f, 0)

        query_and_key_grad(q, k, v, g, probs, slopes, key_total, k_turned, put_query_key, length, block)
        return 0

    lax.fori_loop(0, heads, one_head, 0)

    for w in range(triple):
        far_sent(heads - 1, w)
    sent = pl.ds(0, (groups - 1) * heads)
    pltpu.make_async_copy(own_out.at[:, sent], own_out.at[:, sent], own_send).wait()
    pltpu.make_async_copy(grad_out.at[sent], grad_out.at[sent], grad_send).wait()
    rest = pl.ds(1, groups - 1)
    pltpu.make_async_copy(out.at[rest], out.at[rest], out_send).wait()
    pltpu.make_async_copy(out, out, out_recv).wait()


def by_token(parts, whole, came, turned, load_sem, store_sem):
    groups, heads, triple, tokens, width = parts.shape
    step = 16
    chunk = tokens // 4
    chunks = [(c, w) for c in range(tokens // chunk) for w in range(triple)]
    loads, stores = [], []
    for at, (c, w) in enumerate(chunks):
        rows = pl.ds(c * chunk, chunk)
        loads.append(pltpu.make_async_copy(parts.at[:, :, w, rows], came.at[c, w], load_sem.at[at]))
        stores.append(pltpu.make_async_copy(turned.at[c, w], whole.at[rows, w], store_sem.at[at]))
    for load in loads:
        load.start()
    for at, (c, w) in enumerate(chunks):
        loads[at].wait()
        for n in range(chunk // step):
            rows = pl.ds(n * step, step)
            piece = came[c, w, :, :, rows, :].reshape(groups * heads, step, width)
            turned[c, w, rows] = jnp.swapaxes(piece, 0, 1)
        stores[at].start()
    for store in stores:
        store.wait()


def solution(mesh):
    sections, groups = mesh.shape["section"], mesh.shape["tp"]

    def local(saved_caches, keeper_code, result_slope):
        slots, tokens, triple, head_count, width = saved_caches.shape[1:]
        heads = head_count // groups
        length = groups * tokens
        block = 256
        blocks = length // block
        anywhere = pl.BlockSpec(memory_space=pl.ANY)
        vmem = pltpu.VMEM
        sem = pltpu.SemaphoreType.DMA
        out = pl.pallas_call(
            functools.partial(kernel, sections, groups, heads, tokens, block, slots),
            out_shape=jax.ShapeDtypeStruct((groups, heads, triple, tokens, width), BF16),
            in_specs=[pl.BlockSpec(memory_space=pltpu.SMEM), anywhere, anywhere],
            out_specs=anywhere,
            scratch_shapes=[
                *[vmem((slots, tokens, head_count, width), BF16)] * triple,
                vmem((tokens, head_count, width), BF16),
                vmem((triple, head_count, tokens, width), BF16),
                vmem((triple, head_count, tokens, width), BF16),
                vmem((head_count, tokens, width), BF16),
                vmem((heads, triple, length, width), BF16),
                vmem((heads, triple, length, width), BF16),
                vmem((heads, length, width), BF16),
                vmem((triple, length, width), BF16),
                vmem((heads, groups, triple, tokens, width), BF16),
                vmem((place(blocks, 0), block, block), F32),
                vmem((2, length, block), F32),
                vmem((length, width), F32),
                vmem((length, width), F32),
                vmem((width, length), BF16),
                pltpu.SemaphoreType.REGULAR,
                sem((triple + 1,)),
                sem((heads, triple)), sem((heads, triple)), sem, sem((heads,)), sem, sem((heads,)), sem, sem,
            ],
            compiler_params=pltpu.CompilerParams(
                collective_id=0, has_side_effects=True, vmem_limit_bytes=56 * 2**20
            ),
        )(keeper_code, saved_caches[0], result_slope[0])
        whole = pl.pallas_call(
            by_token,
            out_shape=jax.ShapeDtypeStruct((tokens, triple, head_count, width), BF16),
            in_specs=[anywhere],
            out_specs=anywhere,
            scratch_shapes=[
                vmem((4, triple, groups, heads, tokens // 4, width), BF16),
                vmem((4, triple, tokens // 4, head_count, width), BF16),
                sem((4 * triple,)), sem((4 * triple,)),
            ],
            compiler_params=pltpu.CompilerParams(vmem_limit_bytes=56 * 2**20),
        )(out)
        return whole[None]

    return jax.shard_map(
        local,
        mesh=mesh,
        in_specs=(P("section", None, "tp", None, None, None), P(), P("section", "tp", None, None)),
        out_specs=P("section", "tp", None, None, None),
        check_vma=False,
    )
```

```python
import functools

import jax
import jax.numpy as jnp
from jax import lax
from jax.experimental import pallas as pl
from jax.experimental.pallas import tpu as pltpu
from jax.sharding import PartitionSpec as P

MESH = pl.DeviceIdType.MESH
F32 = jnp.float32
BF16 = jnp.bfloat16
LOG2E = 1.4426950408889634
ROWS_BY_ROWS = (((1,), (1,)), ((), ()))
PLAIN = (((1,), (0,)), ((), ()))


def dot(a, b, dims):
    return lax.dot_general(a, b, dims, preferred_element_type=F32)


def fold(x, op):
    return op(x.reshape(x.shape[0] // 8, 8, x.shape[1]), axis=0)


def chips_first(n):
    return n % 4 * 2 + n // 4 % 2 + n // 8 * 8


def place(i, j):
    return i * (i + 1) // 2 + j


def softmax_and_value_grad(q, k, g, probs, value_total, put, length, block):
    exponent = q.shape[-1] ** (-0.5) * LOG2E
    blocks = length // block
    key_ids = lax.broadcasted_iota(jnp.int32, (block, block), 0)
    query_ids = lax.broadcasted_iota(jnp.int32, (block, block), 1)
    causal = key_ids <= query_ids
    for i in reversed(range(blocks)):
        rows = pl.ds(i * block, block)
        q_rows, g_rows = q[rows, :], g[rows, :]
        peak = jnp.full((8, block), -3.0e38, F32)
        for j in range(i + 1):
            s = dot(k[pl.ds(j * block, block), :], q_rows, ROWS_BY_ROWS)
            if j == i:
                s = jnp.where(causal, s, F32(-1e30))
            probs[place(i, j)] = s
            peak = jnp.maximum(peak, fold(s, jnp.max))
        peak = jnp.max(peak, axis=0, keepdims=True)
        total = jnp.zeros((8, block), F32)
        for j in range(i + 1):
            e = jnp.exp2((probs[place(i, j)] - peak) * exponent)
            probs[place(i, j)] = e
            total = total + fold(e, jnp.sum)
        inverse = 1.0 / jnp.sum(total, axis=0, keepdims=True)
        for j in range(i + 1):
            cols = pl.ds(j * block, block)
            p = probs[place(i, j)] * inverse
            probs[place(i, j)] = p
            dv = dot(p.astype(BF16), g_rows, PLAIN)
            if i == blocks - 1:
                value_total[cols, :] = dv
            else:
                value_total[cols, :] += dv
        put(i, value_total[rows, :].astype(BF16))


def query_and_key_grad(q, k, v, g, probs, slopes, key_total, k_turned, put, length, block):
    width = q.shape[-1]
    scaling = width ** (-0.5)
    blocks = length // block

    def ahead(i):
        g_rows = g[pl.ds(i * block, block), :]
        dots = jnp.zeros((8, block), F32)
        for j in range(i + 1):
            cols = pl.ds(j * block, block)
            dp = dot(v[cols, :], g_rows, ROWS_BY_ROWS)
            slopes[i % 2, cols, :] = dp
            dots = dots + fold(probs[place(i, j)] * dp, jnp.sum)
        return jnp.sum(dots, axis=0, keepdims=True)

    next_dots = ahead(blocks - 1)
    for i in reversed(range(blocks)):
        rows = pl.ds(i * block, block)
        q_rows = q[rows, :]
        row_dots = next_dots
        if i > 0:
            next_dots = ahead(i - 1)
        query_total = jnp.zeros((width, block), F32)
        for j in range(i + 1):
            cols = pl.ds(j * block, block)
            ds = (probs[place(i, j)] * (slopes[i % 2, cols, :] - row_dots)).astype(BF16)
            dk = dot(ds, q_rows, PLAIN)
            if i == blocks - 1:
                key_total[cols, :] = dk
            else:
                key_total[cols, :] += dk
            query_total = query_total + dot(k_turned[:, cols], ds, PLAIN)
        put(i, (query_total.T * scaling).astype(BF16), (key_total[rows, :] * scaling).astype(BF16))


def kernel(
    sections, groups, heads, tokens, block, slots,
    codes, store, slope, out,
    store_in0, store_in1, store_in2, slope_in, far_out, own_out, grad_out,
    far, own, grad, sel, done, probs, slopes, key_total, value_total, k_turned,
    ready, load_sem, far_send, far_recv, own_send, own_recv, grad_send, grad_recv, out_send, out_recv,
):
    s = lax.axis_index("section")
    t = lax.axis_index("tp")
    mirror = sections - 1 - s
    length = groups * tokens
    triple = store.shape[2]
    mine = pl.ds(pl.multiple_of(t * tokens, tokens), tokens)
    step = 16
    store_in = (store_in0, store_in1, store_in2)

    def load(w):
        return pltpu.make_async_copy(store.at[:, :, w], store_in[w], load_sem.at[w])

    def load_slope():
        return pltpu.make_async_copy(slope, slope_in, load_sem.at[triple])

    for w in (1, 0, 2):
        load(w).start()
    load_slope().start()

    barrier = pltpu.get_barrier_semaphore()

    first = lax.rem(s, 4) < 2
    second = lax.rem(s, 4) >= 2

    def greet(i, _):
        peer = lax.bitwise_xor(t, i)

        @pl.when(i > 0)
        def _():
            pl.semaphore_signal(barrier, inc=1, device_id=(s, peer), device_id_type=MESH)

        pl.semaphore_signal(barrier, inc=1, device_id=(mirror, peer), device_id_type=MESH)
        return 0

    @pl.when(first)
    def _():
        lax.fori_loop(0, groups, greet, 0)

    def answer(i, _):
        pl.semaphore_signal(
            ready, inc=1, device_id=(mirror, lax.bitwise_xor(t, i)), device_id_type=MESH
        )
        return 0

    home = codes[s]
    away = codes[mirror]
    own_slot = jnp.clip(home, 0, slots - 1)
    far_slot = jnp.clip(away - slots, 0, slots - 1)
    take_far = home >= slots

    def by_head(slot, w, to):
        def f(n, _):
            rows = pl.ds(pl.multiple_of(n * step, step), step)
            to[w, :, rows, :] = jnp.swapaxes(store_in[w][slot, rows], 0, 1)
            return 0

        lax.fori_loop(0, tokens // step, f, 0)

    def each_peer(first, f):
        def g(n, _):
            f(lax.bitwise_xor(t, chips_first(n)))
            return 0

        lax.fori_loop(first, groups, g, 0)

    def send_far(hd, w, classes=False):
        def f(peer):
            pltpu.make_async_remote_copy(
                src_ref=far_out.at[w, peer * heads + hd], dst_ref=far.at[hd, w, mine, :],
                send_sem=far_send.at[hd, w], recv_sem=far_recv.at[hd, w],
                device_id=(mirror, peer), device_id_type=MESH,
            ).start()

        if classes:
            def g(n, _):
                order = n // 4
                f(order % 2 * 8 + lax.bitwise_xor(t // 2 % 4, n % 4) * 2 + order // 2)
                return 0

            lax.fori_loop(0, groups, g, 0)
        else:
            each_peer(0, f)

    def far_sent(hd, w):
        some = pl.ds(0, groups)
        pltpu.make_async_copy(far_out.at[w, some], far_out.at[w, some], far_send.at[hd, w]).wait()

    def far_here(hd, w):
        pltpu.make_async_copy(far.at[hd, w], far.at[hd, w], far_recv.at[hd, w]).wait()

    def send_own(hd):
        pltpu.make_async_copy(own_out.at[:, t * heads + hd], own.at[hd, :, mine, :], own_recv.at[hd]).start()
        pltpu.make_async_copy(grad_out.at[t * heads + hd], grad.at[hd, mine, :], grad_recv.at[hd]).start()

        def f(peer):
            pltpu.make_async_remote_copy(
                src_ref=own_out.at[:, peer * heads + hd], dst_ref=own.at[hd, :, mine, :],
                send_sem=own_send, recv_sem=own_recv.at[hd],
                device_id=(s, peer), device_id_type=MESH,
            ).start()
            pltpu.make_async_remote_copy(
                src_ref=grad_out.at[peer * heads + hd], dst_ref=grad.at[hd, mine, :],
                send_sem=grad_send, recv_sem=grad_recv.at[hd],
                device_id=(s, peer), device_id_type=MESH,
            ).start()

        each_peer(1, f)

    late = pl.ds(triple - 1, 1)
    early = pl.ds(0, triple - 1)
    last = triple - 1

    def slope_by_head(n, _):
        rows = pl.ds(pl.multiple_of(n * step, step), step)
        grad_out[:, rows, :] = jnp.swapaxes(slope_in[rows], 0, 1)
        return 0

    @pl.when(second)
    def _():
        pl.semaphore_wait(barrier, groups)
        lax.fori_loop(0, groups, answer, 0)

    load(1).wait()
    by_head(far_slot, 1, far_out)

    @pl.when(second)
    def _():
        send_far(0, 1)

    load(0).wait()
    load(last).wait()
    load_slope().wait()
    for w in range(triple):
        by_head(own_slot, w, own_out)
    lax.fori_loop(0, tokens // step, slope_by_head, 0)

    @pl.when(first)
    def _():
        pl.semaphore_wait(barrier, groups - 1)

    by_head(far_slot, 0, far_out)

    @pl.when(second)
    def _():
        send_far(0, 0)
        pl.semaphore_wait(ready, 1)

    send_own(0)
    by_head(far_slot, last, far_out)

    @pl.when(first)
    def _():
        for hd in range(1, heads):
            send_own(hd)
        pl.semaphore_wait(ready, groups)
        pl.semaphore_signal(ready, inc=1, device_id=(mirror, t), device_id_type=MESH)
        send_far(0, 1)
        send_far(0, 0)

    send_far(0, last)

    @pl.when(second)
    def _():
        for hd in range(1, heads):
            send_own(hd)

    far_sent(0, 1)
    send_far(1, 1)
    far_sent(0, 0)
    send_far(1, 0)

    def one_head(hd, _):
        pltpu.make_async_copy(own.at[hd], own.at[hd], own_recv.at[hd]).wait()
        pltpu.make_async_copy(grad.at[hd], grad.at[hd], grad_recv.at[hd]).wait()
        far_here(hd, 1)
        far_here(hd, 0)

        def choose(ws):
            def f(n, _):
                rows = pl.ds(pl.multiple_of(n * block, block), block)
                sel[ws, rows, :] = jnp.where(take_far, far[hd, ws, rows, :], own[hd, ws, rows, :])
                return 0

            lax.fori_loop(0, length // block, f, 0)

        per = block // tokens

        def put_value(i, dv):
            for n in range(per):
                done[hd, i * per + n, 2] = dv[n * tokens:(n + 1) * tokens]

        def give(peer, ws):
            @pl.when(peer == t)
            def _():
                pltpu.make_async_copy(done.at[hd, peer, ws], out.at[t, hd, ws], out_recv).start()

            @pl.when(peer != t)
            def _():
                pltpu.make_async_remote_copy(
                    src_ref=done.at[hd, peer, ws], dst_ref=out.at[t, hd, ws],
                    send_sem=out_send, recv_sem=out_recv,
                    device_id=(s, peer), device_id_type=MESH,
                ).start()

        choose(early)
        q, k, v, g = sel.at[0], sel.at[1], sel.at[2], grad.at[hd]
        k_turned[...] = k[...].T
        softmax_and_value_grad(q, k, g, probs, value_total, put_value, length, block)
        each_peer(0, lambda peer: give(peer, late))

        @pl.when(hd + 1 < heads)
        def _():
            far_sent(hd, last)
            send_far(hd + 1, last, classes=True)

        far_here(hd, last)
        choose(late)
        half = groups // 2

        def put_query_key(i, dq, dk):
            for n in range(per):
                done[hd, i * per + n, 0] = dq[n * tokens:(n + 1) * tokens]
                done[hd, i * per + n, 1] = dk[n * tokens:(n + 1) * tokens]
            if i * per % half == 0:

                def f(n, _):
                    give(i * per + lax.rem(lax.bitwise_xor(t, chips_first(n)), half), early)
                    return 0

                lax.fori_loop(0, half, f, 0)

        query_and_key_grad(q, k, v, g, probs, slopes, key_total, k_turned, put_query_key, length, block)
        return 0

    lax.fori_loop(0, heads, one_head, 0)

    for w in range(triple):
        far_sent(heads - 1, w)
    sent = pl.ds(0, (groups - 1) * heads)
    pltpu.make_async_copy(own_out.at[:, sent], own_out.at[:, sent], own_send).wait()
    pltpu.make_async_copy(grad_out.at[sent], grad_out.at[sent], grad_send).wait()
    rest = pl.ds(1, groups - 1)
    pltpu.make_async_copy(out.at[rest], out.at[rest], out_send).wait()
    pltpu.make_async_copy(out, out, out_recv).wait()


def by_token(parts, whole, came, turned, load_sem, store_sem):
    groups, heads, triple, tokens, width = parts.shape
    step = 16
    chunk = tokens // 4
    chunks = [(c, w) for c in range(tokens // chunk) for w in range(triple)]
    loads, stores = [], []
    for at, (c, w) in enumerate(chunks):
        rows = pl.ds(c * chunk, chunk)
        loads.append(pltpu.make_async_copy(parts.at[:, :, w, rows], came.at[c, w], load_sem.at[at]))
        stores.append(pltpu.make_async_copy(turned.at[c, w], whole.at[rows, w], store_sem.at[at]))
    for load in loads:
        load.start()
    for at, (c, w) in enumerate(chunks):
        loads[at].wait()
        for n in range(chunk // step):
            rows = pl.ds(n * step, step)
            piece = came[c, w, :, :, rows, :].reshape(groups * heads, step, width)
            turned[c, w, rows] = jnp.swapaxes(piece, 0, 1)
        stores[at].start()
    for store in stores:
        store.wait()


def solution(mesh):
    sections, groups = mesh.shape["section"], mesh.shape["tp"]

    def local(saved_caches, keeper_code, result_slope):
        slots, tokens, triple, head_count, width = saved_caches.shape[1:]
        heads = head_count // groups
        length = groups * tokens
        block = 256
        blocks = length // block
        anywhere = pl.BlockSpec(memory_space=pl.ANY)
        vmem = pltpu.VMEM
        sem = pltpu.SemaphoreType.DMA
        out = pl.pallas_call(
            functools.partial(kernel, sections, groups, heads, tokens, block, slots),
            out_shape=jax.ShapeDtypeStruct((groups, heads, triple, tokens, width), BF16),
            in_specs=[pl.BlockSpec(memory_space=pltpu.SMEM), anywhere, anywhere],
            out_specs=anywhere,
            scratch_shapes=[
                *[vmem((slots, tokens, head_count, width), BF16)] * triple,
                vmem((tokens, head_count, width), BF16),
                vmem((triple, head_count, tokens, width), BF16),
                vmem((triple, head_count, tokens, width), BF16),
                vmem((head_count, tokens, width), BF16),
                vmem((heads, triple, length, width), BF16),
                vmem((heads, triple, length, width), BF16),
                vmem((heads, length, width), BF16),
                vmem((triple, length, width), BF16),
                vmem((heads, groups, triple, tokens, width), BF16),
                vmem((place(blocks, 0), block, block), F32),
                vmem((2, length, block), F32),
                vmem((length, width), F32),
                vmem((length, width), F32),
                vmem((width, length), BF16),
                pltpu.SemaphoreType.REGULAR,
                sem((triple + 1,)),
                sem((heads, triple)), sem((heads, triple)), sem, sem((heads,)), sem, sem((heads,)), sem, sem,
            ],
            compiler_params=pltpu.CompilerParams(
                collective_id=0, has_side_effects=True, vmem_limit_bytes=56 * 2**20
            ),
        )(keeper_code, saved_caches[0], result_slope[0])
        whole = pl.pallas_call(
            by_token,
            out_shape=jax.ShapeDtypeStruct((tokens, triple, head_count, width), BF16),
            in_specs=[anywhere],
            out_specs=anywhere,
            scratch_shapes=[
                vmem((4, triple, groups, heads, tokens // 4, width), BF16),
                vmem((4, triple, tokens // 4, head_count, width), BF16),
                sem((4 * triple,)), sem((4 * triple,)),
            ],
            compiler_params=pltpu.CompilerParams(vmem_limit_bytes=56 * 2**20),
        )(out)
        return whole[None]

    return jax.shard_map(
        local,
        mesh=mesh,
        in_specs=(P("section", None, "tp", None, None, None), P(), P("section", "tp", None, None)),
        out_specs=P("section", "tp", None, None, None),
        check_vma=False,
    )
```
